32 devices in a mesh: groups: 2 (over x), gx: 8 (over z, y), yz: 2 (over core).
Axes of the slice: x: 2, y: 2, z: 4, core: 2. Of those that a mesh axis runs over, the one named last changes fastest.
Arguments:
- tokens: bfloat16 [768, 18432], P(('groups', 'yz'), 'gx'), parts along dimension 0, may hold values from -100 to 100
- query_weight: bfloat16 [18432, 6144], P('gx', 'yz'), may hold values from -0.046875 to 0.046875
- keyvalue_weight: bfloat16 [18432, 512], P('gx'), may hold values from -0.046875 to 0.046875
- output_weight: bfloat16 [6144, 18432], P('yz', 'gx'), may hold values from -0.078125 to 0.078125
Outputs:
- attended: bfloat16 [768, 18432], P(('groups', 'yz'), 'gx'), parts along dimension 0
The draws below stay inside these ranges and needn't reach their ends.
There are 2 independent parts, one for each index of `groups`. The reference program is written for one: setup_inputs(seed, part) draws one part's arguments, and reference() takes and returns one part's arrays. A program takes and returns all parts, laid end to end along the dimension named above; an argument that names none is the same for every part. Nothing has to cross between parts.
All inputs are finite; a program needn't handle non-finite values.
Results may differ from the reference program's by a relative error of at most 0.012.
The reference program's roundings to bfloat16 on the way (of `query`, `keyvalue`, `probs` and `mixed`) count: a program that leaves them out, or rounds other values in their place, can miss the bound.
Values may be sent and summed in bfloat16 or wider, within the bound.
No kernel may reach another device: no remote copies, remote signals or barrier semaphores. Data moves between devices by JAX's collectives and lax.ppermute only.
A program may use at most 128 MiB of HBM per device.

```python
import jax
import jax.numpy as jnp

D = 18432
HEADS = 24
HEAD = 256
PROMPT = 384
PROMPTS = 1
TOKENS = 384
QW = 6144


def draw_tokens(key, part):
    key = jax.random.fold_in(key, 11)
    first = jax.random.fold_in(key, 0)
    return jnp.clip(jax.random.normal(first, (TOKENS, D), jnp.float32), -6.0, 6.0).astype(jnp.bfloat16)


def steps_of(rng, shape, cuts, low, largest):
    gain, own = 1.0, jax.random.fold_in(rng, 6)
    for dim, shards_of in cuts:
        steps = jnp.exp(jax.random.uniform(jax.random.fold_in(own, dim), (shards_of,), jnp.float32, low / len(cuts), largest / len(cuts)))
        gain = gain * jnp.repeat(steps, shape[dim] // shards_of).reshape([-1 if axis == dim else 1 for axis in range(len(shape))])
    return gain


def noise(own_key, shape, scale, most, pieces=(), kind=jnp.bfloat16):
    level = steps_of(own_key, shape, pieces, -0.22, 0.18) if pieces else 1.0
    drawn = jax.random.normal(own_key, shape, jnp.float32) * scale * level
    return jnp.minimum(jnp.maximum(drawn, -most), most).astype(kind)


def setup_inputs(seed: int = 0, part: int = 0) -> dict:
    streams_of = jax.random.split(jax.random.key(seed), 5)
    own_keys = jax.random.split(jax.random.fold_in(streams_of[4], part), 5)
    return {
        "tokens": draw_tokens(jax.random.fold_in(jax.random.fold_in(streams_of[4], part), 71), part),
        "query_weight": noise(streams_of[1], (D, QW), D ** -0.5, 0.046875, ((0, 8), (1, 2))),
        "keyvalue_weight": noise(streams_of[2], (D, 2 * HEAD), D ** -0.5, 0.046875, ((0, 8),)),
        "output_weight": noise(streams_of[3], (QW, D), QW ** -0.5, 0.078125, ((0, 2), (1, 8))),
    }


def reference(tokens, query_weight, keyvalue_weight, output_weight):
    query = jnp.dot(tokens, query_weight, preferred_element_type=jnp.float32).astype(jnp.bfloat16)
    keyvalue = jnp.dot(tokens, keyvalue_weight, preferred_element_type=jnp.float32).astype(jnp.bfloat16)
    keys = keyvalue[:, :HEAD].reshape(PROMPT, PROMPTS, HEAD).astype(jnp.float32)
    values = keyvalue[:, HEAD:].reshape(PROMPT, PROMPTS, HEAD).astype(jnp.float32)
    heads_q = query.reshape(PROMPT, PROMPTS, HEADS, HEAD).astype(jnp.float32)
    scores = jnp.einsum("qphd,kpd->pqhk", heads_q, keys) * (HEAD ** -0.5)
    position = jnp.arange(PROMPT)
    allowed = position[None, :] <= position[:, None]
    scores = jnp.where(allowed[None, :, None, :], scores, -1e30)
    probs = jax.nn.softmax(scores, axis=-1).astype(jnp.bfloat16)
    mixed = jnp.einsum("pqhk,kpd->qphd", probs.astype(jnp.float32), values)
    mixed = mixed.astype(jnp.bfloat16).reshape(TOKENS, HEADS * HEAD)
    return jnp.dot(mixed, output_weight, preferred_element_type=jnp.float32).astype(jnp.bfloat16)
```

```python
import jax
import jax.numpy as jnp
from jax import lax
from jax.sharding import PartitionSpec as P

HEAD = 256
PROMPTS = 1
PARTS = 3
F32 = jnp.float32
BF16 = jnp.bfloat16
F16 = jnp.float16
SCALE = 0.5
LOW = 2048.0


def cube(n):
    m = n.bit_length() - 1
    return [1 << j if j < 2 else 3 << (j - 1) for j in range(m)]


def coordinates(index, m):
    bits = [(index >> j) & 1 for j in range(m)]
    out = list(bits)
    for j in range(m - 1, 1, -1):
        out[j - 1] = bits[j - 1] ^ out[j]
    return out


def exchange(x, mask, axis="gx"):
    n = lax.axis_size(axis)
    return lax.ppermute(x, axis, [(i, i ^ mask) for i in range(n)])


def split(x):
    half = x * SCALE
    high = lax.reduce_precision(half, 5, 10)
    low = (half - high) * LOW
    return jnp.concatenate([high.astype(F16), low.astype(F16)], axis=-1)


def join(x):
    c = x.shape[-1] // 2
    return (x[..., :c].astype(F32) + x[..., c:].astype(F32) * (1.0 / LOW)) * (1.0 / SCALE)


def pick(x, at, axis):
    return lax.dynamic_index_in_dim(x, at, axis, keepdims=False)


def on_device(tokens, query_weight, keyvalue_weight, output_weight):
    n = lax.axis_size("gx")
    masks = cube(n)
    m = len(masks)
    core = lax.axis_index("yz")
    where = coordinates(lax.axis_index("gx"), m)
    own = tokens.shape[0]
    total = own * lax.axis_size("yz")
    span = total // n
    width = query_weight.shape[1]
    cols = width // PARTS
    other = exchange(tokens, 1, "yz")
    kv = jnp.dot(tokens, keyvalue_weight, preferred_element_type=F32)
    whole = jnp.where(
        core == 0, jnp.concatenate([tokens, other], 0), jnp.concatenate([other, tokens], 0)
    )
    cubed = whole.reshape([2] * m + [span, whole.shape[1]])
    orders = [[(p * m // PARTS + j) % m for j in range(m)] for p in range(PARTS)]

    kvs = [kv[p * (own // PARTS) : (p + 1) * (own // PARTS)] for p in range(PARTS)]
    kept, got = [], []
    for p in range(PARTS):
        d = orders[p][0]
        w = query_weight[:, p * cols : (p + 1) * cols]
        rows = pick(cubed, 1 - where[d], d).reshape(total // 2, -1)
        send = (jnp.dot(rows, w, preferred_element_type=F32) * SCALE).astype(F16)
        got.append(exchange(jnp.concatenate([send, split(kvs[p])], 0), masks[d]))
    for p in range(PARTS):
        d = orders[p][0]
        w = query_weight[:, p * cols : (p + 1) * cols]
        rows = pick(cubed, where[d], d).reshape(total // 2, -1)
        kept.append(jnp.dot(rows, w, preferred_element_type=F32))
    left = [sorted(set(range(m)) - {orders[p][0]}) for p in range(PARTS)]
    for s in range(1, m + 1):
        for p in range(PARTS):
            size = kept[p].shape[0]
            kept[p] = kept[p] + got[p][:size].astype(F32) * (1.0 / SCALE)
            kvs[p] = kvs[p] + join(got[p][size:])
        if s == m:
            break
        for p in range(PARTS):
            d = orders[p][s]
            axis = left[p].index(d)
            left[p].remove(d)
            x = kept[p].reshape([2] * (m - s) + [span, cols])
            send = (pick(x, 1 - where[d], axis).reshape(-1, cols) * SCALE).astype(F16)
            kept[p] = pick(x, where[d], axis).reshape(-1, cols)
            got[p] = exchange(jnp.concatenate([send, split(kvs[p])], 0), masks[d])

    block = sum(where[d] << (m - 1 - d) for d in range(m))
    own_kv = jnp.concatenate(kvs, 0).astype(BF16)
    other_kv = exchange(own_kv, 1, "yz")
    keyvalue = jnp.where(
        core == 0, jnp.concatenate([own_kv, other_kv], 0), jnp.concatenate([other_kv, own_kv], 0)
    )
    keys = keyvalue[:, :HEAD]
    values = keyvalue[:, HEAD:]
    heads = cols // HEAD
    query_pos = block * span + jnp.arange(span)
    key_pos = jnp.arange(total)
    allowed = (key_pos[None, :] <= query_pos[:, None]) & (
        key_pos[None, :] % PROMPTS == query_pos[:, None] % PROMPTS
    )
    mixed = []
    for p in range(PARTS):
        grouped = kept[p].astype(BF16).reshape(span, heads, HEAD)
        scores = jnp.einsum("qhd,kd->hqk", grouped, keys, preferred_element_type=F32) * HEAD ** (
            -0.5
        )
        scores = jnp.where(allowed[None], scores, -1e30)
        probs = lax.optimization_barrier(jax.nn.softmax(scores, axis=-1).astype(BF16))
        out = jnp.einsum("hqk,kd->qhd", probs, values, preferred_element_type=F32)
        mixed.append(out.astype(BF16).reshape(span, cols))

    have = [[] for _ in range(PARTS)]
    for s in range(m - 1, -1, -1):
        received = [exchange(mixed[p], masks[orders[p][s]]) for p in range(PARTS)]
        for p in range(PARTS):
            d = orders[p][s]
            have[p] = sorted(have[p] + [d])
            axis = have[p].index(d)
            shape = [2] * (len(have[p]) - 1) + [span, cols]
            a, b = mixed[p].reshape(shape), received[p].reshape(shape)
            low, high = jnp.where(where[d] == 0, a, b), jnp.where(where[d] == 0, b, a)
            mixed[p] = jnp.stack([low, high], axis).reshape(-1, cols)
    mixed = jnp.concatenate(mixed, 1)
    theirs = lax.dynamic_slice_in_dim(mixed, (1 - core) * own, own, 0)
    mine = lax.dynamic_slice_in_dim(mixed, core * own, own, 0)
    send = jnp.dot(theirs, output_weight, preferred_element_type=F32)
    back = exchange(send, 1, "yz")
    return (jnp.dot(mine, output_weight, preferred_element_type=F32) + back).astype(BF16)


def solution(mesh):
    return jax.shard_map(
        on_device,
        mesh=mesh,
        in_specs=(P(("groups", "yz"), "gx"), P("gx", "yz"), P("gx", None), P("yz", "gx")),
        out_specs=P(("groups", "yz"), "gx"),
        check_vma=False,
    )
```

```python
import jax
import jax.numpy as jnp
from jax import lax
from jax.sharding import PartitionSpec as P

HEAD = 256
PROMPTS = 1
GROUPS = 2
CHUNKS = 2
F32 = jnp.float32
BF16 = jnp.bfloat16
F16 = jnp.float16
SCALE = 0.5


def exchange(x, bit, axis="gx"):
    n = lax.axis_size(axis)
    return lax.ppermute(x, axis, [(i, i ^ (1 << bit)) for i in range(n)])


def pick(x, at, axis):
    return lax.dynamic_index_in_dim(x, at, axis, keepdims=False)


def half(x):
    return (x * SCALE).astype(F16)


def full(x):
    return x.astype(F32) * (1.0 / SCALE)


def on_device(tokens, query_weight, keyvalue_weight, output_weight):
    n = lax.axis_size("gx")
    m = n.bit_length() - 1
    core = lax.axis_index("yz")
    place = lax.axis_index("gx")
    where = [(place >> j) & 1 for j in range(m)]
    own = tokens.shape[0]
    total = 2 * own
    small = own // n
    span = 2 * small
    width = query_weight.shape[1]
    cols = width // (2 * GROUPS)
    orders = ((0, 1), (1, 0))

    def both(a, b, d, axis):
        first = where[d] == 0
        return jnp.stack([jnp.where(first, a, b), jnp.where(first, b, a)], axis)

    cube = [2] * m + [small]
    other = exchange(tokens, 0, "yz")
    kv = jnp.dot(tokens, keyvalue_weight, preferred_element_type=F32).reshape(cube + [-1])

    def kv_chain(x):
        for d in range(m - 1):
            got = exchange(pick(x, 1 - where[d], 0), d)
            x, got = yield pick(x, where[d], 0), got
            x = x + got
        x, got = yield x, exchange(x, m - 1)
        x = (x + got).astype(BF16)
        for d in range(m - 2, -1, -1):
            x, got = yield x, exchange(x, d)
            x = both(x, got, d, 0)
        x = x.reshape(own, 2 * HEAD)
        x, got = yield x, exchange(x, 0, "yz")
        return jnp.concatenate([x, got], 0)

    whole = jnp.stack([tokens, other]).reshape([2] + cube + [tokens.shape[1]])

    def product(g, part, mine):
        d = orders[part][0]
        first = (2 * g + part) * cols
        rows = pick(whole, where[d] if mine else 1 - where[d], 1 + d)
        return jnp.dot(
            rows.reshape(total // 2, -1),
            query_weight[:, first : first + cols],
            preferred_element_type=F32,
        )

    def query_chain(g):
        got = [exchange(half(product(g, part, False)), orders[part][0]) for part in range(2)]
        kept = [product(g, part, True) for part in range(2)]
        kept, got = yield kept, got
        after = []
        for part in range(2):
            x = (kept[part] + full(got[part])).reshape([2] * m + [small, cols])
            d = orders[part][1]
            got[part] = exchange(half(pick(x, 1 - where[d], 1)), d)
            after.append(pick(x, where[d], 1))
        kept, got = yield after, got
        x = jnp.concatenate([k + full(r) for k, r in zip(kept, got)], -1)
        for d in range(2, m):
            got = exchange(half(pick(x, 1 - where[d], 1)), d)
            x, got = yield pick(x, where[d], 1), got
            x = x + full(got)
        return x.astype(BF16)

    def attention(query, keyvalue):
        positions = jnp.arange(own)
        key_pos = jnp.concatenate([positions + core * own, positions + (1 - core) * own])
        block = sum(where[d] << (m - 1 - d) for d in range(m))
        query_pos = block * small + jnp.arange(small)
        query_pos = jnp.concatenate([query_pos + core * own, query_pos + (1 - core) * own])
        allowed = (key_pos[None, :] <= query_pos[:, None]) & (
            key_pos[None, :] % PROMPTS == query_pos[:, None] % PROMPTS
        )
        grouped = query.reshape(span, -1, HEAD)
        scores = jnp.einsum("qhd,kd->hqk", grouped, keyvalue[:, :HEAD], preferred_element_type=F32)
        scores = jnp.where(allowed[None], scores * HEAD ** (-0.5), -1e30)
        probs = lax.optimization_barrier(jax.nn.softmax(scores, axis=-1).astype(BF16))
        out = jnp.einsum("hqk,kd->qhd", probs, keyvalue[:, HEAD:], preferred_element_type=F32)
        return out.astype(BF16).reshape(2, small, 2 * cols)

    def mixed_chain(x):
        for d in range(m - 1, 1, -1):
            x, got = yield x, exchange(x, d)
            x = both(x, got, d, 1)
        parts = [x[..., :cols], x[..., cols:]]
        got = [exchange(parts[part], orders[part][1]) for part in range(2)]
        parts, got = yield parts, got
        parts = [both(parts[part], got[part], orders[part][1], 1) for part in range(2)]
        got = [exchange(parts[part], orders[part][0]) for part in range(2)]
        parts, got = yield parts, got
        parts = [both(parts[part], got[part], orders[part][0], 1 + orders[part][0]) for part in range(2)]
        return jnp.concatenate([x.reshape(total, cols) for x in parts], 1)

    class Chain:
        def __init__(self, chain):
            self.chain, self.done = chain, None
            self.state = next(chain)

        def go(self, *others):
            made = [o.state[0] for o in others]
            state, made = lax.optimization_barrier((self.state, made))
            for o, x in zip(others, made):
                o.state = (x, o.state[1])
            try:
                self.state = self.chain.send(state)
            except StopIteration as stop:
                self.done = stop.value

    k = Chain(kv_chain(kv))
    a, b = (Chain(query_chain(g)) for g in range(GROUPS))
    steps = m
    k.go(a, b)
    a.go(k, b)
    for s in range(1, steps):
        k.go(a, b)
        b.go(k, a)
        k.go(a, b)
        a.go(k, b)
    while k.done is None:
        k.go(b)
    a_mixed = Chain(mixed_chain(attention(a.done, k.done)))
    b.go(a_mixed)
    b_mixed = Chain(mixed_chain(attention(b.done, k.done)))
    for s in range(steps):
        a_mixed.go(b_mixed)
        if s < steps - 1:
            b_mixed.go(a_mixed)
    depth = 2 * cols
    early = jnp.dot(a_mixed.done, output_weight[:depth], preferred_element_type=F32)
    b_mixed.state, early = lax.optimization_barrier((b_mixed.state, early))
    b_mixed.go()
    outs = []
    wide = output_weight.shape[1] // CHUNKS
    for c in range(CHUNKS):
        at = slice(c * wide, (c + 1) * wide)
        part = early[:, at] + jnp.dot(
            b_mixed.done, output_weight[depth:, at], preferred_element_type=F32
        )
        outs.append((part[:own] + exchange(part[own:], 0, "yz")).astype(BF16))
    return jnp.concatenate(outs, 1)


def solution(mesh):
    return jax.shard_map(
        on_device,
        mesh=mesh,
        in_specs=(P(("groups", "yz"), "gx"), P("gx", "yz"), P("gx", None), P("yz", "gx")),
        out_specs=P(("groups", "yz"), "gx"),
        check_vma=False,
    )
```

```python
import jax
import jax.numpy as jnp
from jax import lax
from jax.sharding import PartitionSpec as P

HEAD = 256
PROMPTS = 1
GROUPS = 2
F32 = jnp.float32
BF16 = jnp.bfloat16
F16 = jnp.float16
SCALE = 0.5


def to_other_core(x):
    return lax.ppermute(x, "yz", [(0, 1), (1, 0)])


def pick(x, at, axis):
    return lax.dynamic_index_in_dim(x, at, axis, keepdims=False)


def half(x):
    return (x * SCALE).astype(F16)


def full(x):
    return x.astype(F32) * (1.0 / SCALE)


def after(x, *made):
    return lax.optimization_barrier((x, made))[0]


def on_device(tokens, query_weight, keyvalue_weight, output_weight):
    n = lax.axis_size("gx")
    m = n.bit_length() - 1
    core = lax.axis_index("yz")
    place = lax.axis_index("gx")
    own = tokens.shape[0]
    total = 2 * own
    small = own // n
    span = 2 * small
    width = query_weight.shape[1]
    cols = width // GROUPS

    def bit(d, c):
        return d if d > 1 else d ^ c

    def exchange(x, d):
        pairs = [(2 * i + c, 2 * (i ^ (1 << bit(d, c))) + c) for i in range(n) for c in range(2)]
        return lax.ppermute(x, ("gx", "yz"), pairs)

    bits = [(place >> j) & 1 for j in range(m)]
    where = [jnp.where(core == 0, bits[d], bits[bit(d, 1)]) for d in range(m)]

    def both(a, b, d, axis):
        first = where[d] == 0
        return jnp.stack([jnp.where(first, a, b), jnp.where(first, b, a)], axis)

    cube = [2] * m + [small]
    other = to_other_core(tokens)
    kv = jnp.dot(tokens, keyvalue_weight, preferred_element_type=F32).reshape(cube + [-1])

    def kv_chain(x):
        for d in range(m - 1):
            sent = pick(x, 1 - where[d], 0)
            x, got = yield pick(x, where[d], 0), sent, exchange(sent, d)
            x = x + got
        x, got = yield x, x, exchange(x, m - 1)
        x = (x + got).astype(BF16)
        for d in range(m - 2, -1, -1):
            x, got = yield x, x, exchange(x, d)
            x = both(x, got, d, 0)
        x = x.reshape(own, 2 * HEAD)
        x, got = yield x, x, to_other_core(x)
        return jnp.concatenate([x, got], 0)

    whole = jnp.stack([tokens, other]).reshape([2] + cube + [tokens.shape[1]])

    def product(rows, g, at):
        return jnp.dot(
            pick(rows, at, 1).reshape(total // 2, -1),
            query_weight[:, g * cols : (g + 1) * cols],
            preferred_element_type=F32,
        )

    def query_chain(g, rows):
        sent = half(product(rows, g, 1 - where[0]))
        x, got = yield None, sent, exchange(sent, 0)
        x = (x + full(got)).reshape([2] * m + [small, cols])
        for d in range(1, m):
            sent = half(pick(x, 1 - where[d], 1))
            x, got = yield pick(x, where[d], 1), sent, exchange(sent, d)
            x = x + full(got)
        return x.astype(BF16)

    def attention(query, keyvalue):
        positions = jnp.arange(own)
        key_pos = jnp.concatenate([positions + core * own, positions + (1 - core) * own])
        block = sum(where[d] << (m - 1 - d) for d in range(m))
        query_pos = block * small + jnp.arange(small)
        query_pos = jnp.concatenate([query_pos + core * own, query_pos + (1 - core) * own])
        allowed = (key_pos[None, :] <= query_pos[:, None]) & (
            key_pos[None, :] % PROMPTS == query_pos[:, None] % PROMPTS
        )
        grouped = query.reshape(span, -1, HEAD)
        scores = jnp.einsum("qhd,kd->hqk", grouped, keyvalue[:, :HEAD], preferred_element_type=F32)
        scores = jnp.where(allowed[None], scores * HEAD ** (-0.5), -1e30)
        probs = lax.optimization_barrier(jax.nn.softmax(scores, axis=-1).astype(BF16))
        out = jnp.einsum("hqk,kd->qhd", probs, keyvalue[:, HEAD:], preferred_element_type=F32)
        return out.astype(BF16).reshape(2, small, cols)

    def mixed_chain(x):
        for d in range(m - 1, -1, -1):
            x, got = yield x, x, exchange(x, d)
            x = both(x, got, d, 1)
        return x.reshape(total, cols)

    class Chain:
        def __init__(self, chain):
            self.chain, self.done = chain, None
            self.kept, self.sent, self.got = next(chain)

        def go(self, *made):
            kept, got = after((self.kept, self.got), *made)
            try:
                self.kept, self.sent, self.got = self.chain.send((kept, got))
            except StopIteration as stop:
                self.done = self.sent = stop.value

    class Sequence:
        def __init__(self):
            self.last = ()

        def go(self, chain, *made):
            chain.go(self.last, *made)
            self.last = chain.sent

        def open(self, chain):
            self.last = chain.sent
            return chain

        def rows(self):
            return after(whole, self.last)

    line = Sequence()
    k = line.open(Chain(kv_chain(kv)))
    q = [None] * GROUPS

    def send(g):
        q[g] = line.open(Chain(query_chain(g, line.rows())))

    def keep(g):
        q[g].kept = line.last = product(line.rows(), g, where[0])

    o = [None] * GROUPS

    def attend(g):
        line.go(q[g])
        o[g] = line.open(Chain(mixed_chain(attention(q[g].done, k.done))))

    def feed():
        if k.done is None:
            line.go(k)

    send(0)
    feed()
    for g in range(1, GROUPS):
        send(g)
        feed()
    for g in range(GROUPS):
        keep(g)
    waves = [(w, w - g, g) for w in range(1, m + GROUPS) for g in range(GROUPS - 1, -1, -1)]
    for w, s, g in waves:
        if 1 <= s < m:
            line.go(q[g])
            feed()
        elif s == m:
            while k.done is None:
                feed()
            attend(g)
    for s in range(1, m):
        for g in range(GROUPS):
            line.go(o[g])
    for g in range(GROUPS - 1):
        line.go(o[g])
    depth = (GROUPS - 1) * cols
    early = jnp.concatenate([x.done for x in o[:-1]], 1)
    early = jnp.dot(early, output_weight[:depth], preferred_element_type=F32)
    ours = early[:own] + to_other_core(early[own:])
    line.last = early
    line.go(o[-1])
    rest = o[-1].done
    theirs = jnp.dot(rest[own:], output_weight[depth:], preferred_element_type=F32).astype(BF16)
    came = to_other_core(theirs)
    rest = after(rest[:own], theirs)
    ours = ours + jnp.dot(rest, output_weight[depth:], preferred_element_type=F32)
    return (after(ours, came) + came.astype(F32)).astype(BF16)


def solution(mesh):
    return jax.shard_map(
        on_device,
        mesh=mesh,
        in_specs=(P(("groups", "yz"), "gx"), P("gx", "yz"), P("gx", None), P("yz", "gx")),
        out_specs=P(("groups", "yz"), "gx"),
        check_vma=False,
    )
```

```python
import jax
import jax.numpy as jnp
from jax import lax
from jax.experimental import pallas as pl
from jax.experimental.pallas import tpu as pltpu
from jax.sharding import PartitionSpec as P

HEAD = 256
PROMPTS = 1
GROUPS = 2
F32 = jnp.float32
BF16 = jnp.bfloat16
F16 = jnp.float16
SCALE = 0.5


def to_other_core(x):
    return lax.ppermute(x, "yz", [(0, 1), (1, 0)])


def pick(x, at, axis):
    return lax.dynamic_index_in_dim(x, at, axis, keepdims=False)


def half(x):
    return (x * SCALE).astype(F16)


def full(x):
    return x.astype(F32) * (1.0 / SCALE)


def halves_kernel(at, x, w, sent, kept, rows, near, sem):
    size = sent.shape[0]
    copies = [
        pltpu.make_async_copy(
            x.at[pl.ds(pl.multiple_of(half_of * size, size), size)],
            rows.at[pl.ds(i * size, size)],
            sem.at[i],
        )
        for i, half_of in enumerate((1 - at[0], at[0]))
    ]
    copies.append(pltpu.make_async_copy(w, near, sem.at[2]))
    for copy in copies:
        copy.start()
    for copy in copies:
        copy.wait()
    out = jnp.dot(rows[...], near[...], preferred_element_type=F32)
    sent[...] = out[:size]
    kept[...] = out[size:]


def halves(x, w, at):
    out = jax.ShapeDtypeStruct((x.shape[0] // 2, w.shape[1]), F32)
    anywhere, vmem = pl.BlockSpec(memory_space=pl.ANY), pl.BlockSpec(memory_space=pltpu.VMEM)
    return pl.pallas_call(
        halves_kernel,
        out_shape=[out, out],
        in_specs=[pl.BlockSpec(memory_space=pltpu.SMEM), anywhere, anywhere],
        out_specs=[vmem, vmem],
        scratch_shapes=[
            pltpu.VMEM(x.shape, x.dtype),
            pltpu.VMEM(w.shape, w.dtype),
            pltpu.SemaphoreType.DMA((3,)),
        ],
        compiler_params=pltpu.CompilerParams(vmem_limit_bytes=56 << 20),
        cost_estimate=pl.CostEstimate(
            flops=2 * x.size * w.shape[1], bytes_accessed=2 * (x.size + w.size), transcendentals=0
        ),
    )(at.astype(jnp.int32).reshape(1), x, w)


def after(x, *made):
    return lax.optimization_barrier((x, made))[0]


def on_device(tokens, query_weight, keyvalue_weight, output_weight):
    n = lax.axis_size("gx")
    m = n.bit_length() - 1
    core = lax.axis_index("yz")
    place = lax.axis_index("gx")
    own = tokens.shape[0]
    total = 2 * own
    small = own // n
    span = 2 * small
    width = query_weight.shape[1]
    cols = width // GROUPS

    def bit(d, c):
        return d if d > 1 else d ^ c

    def exchange(x, d):
        pairs = [(2 * i + c, 2 * (i ^ (1 << bit(d, c))) + c) for i in range(n) for c in range(2)]
        return lax.ppermute(x, ("gx", "yz"), pairs)

    bits = [(place >> j) & 1 for j in range(m)]
    where = [jnp.where(core == 0, bits[d], bits[bit(d, 1)]) for d in range(m)]

    def both(a, b, d, axis):
        first = where[d] == 0
        return jnp.stack([jnp.where(first, a, b), jnp.where(first, b, a)], axis)

    cube = [2] * m + [small]
    other = to_other_core(tokens)

    def kv_chain():
        sent, x = halves(tokens, keyvalue_weight, where[0])
        x, got = yield x, sent, exchange(sent, 0)
        x = (x + got).reshape(cube[1:] + [2 * HEAD])
        for d in range(1, m - 1):
            sent = pick(x, 1 - where[d], 0)
            x, got = yield pick(x, where[d], 0), sent, exchange(sent, d)
            x = x + got
        x, got = yield x, x, exchange(x, m - 1)
        x = (x + got).astype(BF16)
        for d in range(m - 2, -1, -1):
            x, got = yield x, x, exchange(x, d)
            x = both(x, got, d, 0)
        x = x.reshape(own, 2 * HEAD)
        x, got = yield x, x, to_other_core(x)
        return jnp.concatenate([x, got], 0)

    whole = jnp.stack([tokens, other]).reshape([2] + cube + [tokens.shape[1]])

    def product(rows, g, at):
        return jnp.dot(
            pick(rows, at, 1).reshape(total // 2, -1),
            query_weight[:, g * cols : (g + 1) * cols],
            preferred_element_type=F32,
        )

    def query_chain(g, rows):
        sent = half(product(rows, g, 1 - where[0]))
        x, got = yield None, sent, exchange(sent, 0)
        x = (x + full(got)).reshape([2] * m + [small, cols])
        for d in range(1, m):
            sent = half(pick(x, 1 - where[d], 1))
            x, got = yield pick(x, where[d], 1), sent, exchange(sent, d)
            x = x + full(got)
        return x.astype(BF16)

    def attention(query, keyvalue):
        positions = jnp.arange(own)
        key_pos = jnp.concatenate([positions + core * own, positions + (1 - core) * own])
        block = sum(where[d] << (m - 1 - d) for d in range(m))
        query_pos = block * small + jnp.arange(small)
        query_pos = jnp.concatenate([query_pos + core * own, query_pos + (1 - core) * own])
        allowed = (key_pos[None, :] <= query_pos[:, None]) & (
            key_pos[None, :] % PROMPTS == query_pos[:, None] % PROMPTS
        )
        grouped = query.reshape(span, -1, HEAD)
        scores = jnp.einsum("qhd,kd->hqk", grouped, keyvalue[:, :HEAD], preferred_element_type=F32)
        scores = jnp.where(allowed[None], scores * HEAD ** (-0.5), -1e30)
        probs = lax.optimization_barrier(jax.nn.softmax(scores, axis=-1).astype(BF16))
        out = jnp.einsum("hqk,kd->qhd", probs, keyvalue[:, HEAD:], preferred_element_type=F32)
        return out.astype(BF16).reshape(2, small, cols)

    def mixed_chain(x):
        for d in range(m - 1, -1, -1):
            x, got = yield x, x, exchange(x, d)
            x = both(x, got, d, 1)
        return x.reshape(total, cols)

    class Chain:
        def __init__(self, chain):
            self.chain, self.done = chain, None
            self.kept, self.sent, self.got = next(chain)

        def go(self, *made):
            kept, got = after((self.kept, self.got), *made)
            try:
                self.kept, self.sent, self.got = self.chain.send((kept, got))
            except StopIteration as stop:
                self.done = self.sent = stop.value

    class Sequence:
        def __init__(self):
            self.last = ()

        def go(self, chain, *made):
            chain.go(self.last, *made)
            self.last = chain.sent

        def open(self, chain):
            self.last = chain.sent
            return chain

        def rows(self):
            return after(whole, self.last)

    line = Sequence()
    k = line.open(Chain(kv_chain()))
    q = [None] * GROUPS

    def send(g):
        q[g] = line.open(Chain(query_chain(g, line.rows())))

    def keep(g):
        q[g].kept = line.last = product(line.rows(), g, where[0])

    o = [None] * GROUPS

    def attend(g):
        line.go(q[g])
        o[g] = line.open(Chain(mixed_chain(attention(q[g].done, k.done))))

    def feed():
        if k.done is None:
            line.go(k)

    for g in range(GROUPS):
        send(g)
        feed()
        keep(g)
    for s in range(1, m):
        for g in range(GROUPS):
            line.go(q[g])
            feed()
    while k.done is None:
        feed()
    for g in range(GROUPS):
        attend(g)
    for s in range(1, m):
        for g in range(GROUPS):
            line.go(o[g])
    for g in range(GROUPS - 1):
        line.go(o[g])
    depth = (GROUPS - 1) * cols
    early = jnp.concatenate([x.done for x in o[:-1]], 1)
    early = jnp.dot(early, output_weight[:depth], preferred_element_type=F32)
    line.last = early
    line.go(o[-1])
    rest = o[-1].done
    theirs = jnp.dot(rest[own:], output_weight[depth:], preferred_element_type=F32)
    theirs = (early[own:] + theirs).astype(BF16)
    came = to_other_core(theirs)
    rest = after(rest[:own], theirs)
    ours = early[:own] + jnp.dot(rest, output_weight[depth:], preferred_element_type=F32)
    return (after(ours, came) + came.astype(F32)).astype(BF16)


def solution(mesh):
    return jax.shard_map(
        on_device,
        mesh=mesh,
        in_specs=(P(("groups", "yz"), "gx"), P("gx", "yz"), P("gx", None), P("yz", "gx")),
        out_specs=P(("groups", "yz"), "gx"),
        check_vma=False,
    )
```
